256 devices in a mesh: tensor: 4 (over y), req: 64 (over x, z, core).
Axes of the slice: x: 4, y: 4, z: 8, core: 2. Of those that a mesh axis runs over, the one named last changes fastest.
Arguments:
- hidden_in: bfloat16 [256, 8192], P('req')
- attn_gain: float32 [8192], replicated, may hold values from 0.25 to 1.75
- w_query: bfloat16 [8192, 8192], P('req', 'tensor')
- w_keyval: bfloat16 [2, 8192, 1024], P(None, 'req', 'tensor')
- w_output: bfloat16 [8192, 8192], P('tensor', 'req')
- final_gain: float32 [8192], replicated, may hold values from 0.25 to 1.75
- w_head: bfloat16 [8192, 32000], P('tensor', 'req')
- cache_keys: bfloat16 [256, 2048, 8, 128], P('req', None, 'tensor')
- cache_values: bfloat16 [256, 2048, 8, 128], P('req', None, 'tensor'), may hold values from -6 to 6
- cache_lengths: int32 [256], P('req'), may hold values from 256 to 2047, as said below
- premature: bfloat16 [4, 256, 8192], P(None, 'req')
- premature_layer: int32 [256], P('req'), may hold values from 0 to 3
Outputs:
- contrast: float32 [256, 32000], P('tensor', 'req')
The draws below stay inside these ranges and needn't reach their ends.
Inputs may be any that keep to these rules, and one draw needn't show every extreme that they name: `cache_lengths`: at least 256; some request has exactly 2047.
All inputs are finite; a program needn't handle non-finite values.
Results may differ from the reference program's by a relative error of at most 0.012.
The reference program's roundings to bfloat16 on the way (of `normed`, `weights`, `attended`, `final_rows` and `early_rows`) count: a program that leaves them out, or rounds other values in their place, can miss the bound.
Values may be sent and summed in bfloat16 or wider, within the bound.
No kernel may reach another device: no remote copies, remote signals or barrier semaphores. Data moves between devices by JAX's collectives and lax.ppermute only.
A program may use at most 64 MiB of HBM per device.

```python
import math
import jax
import jax.numpy as jnp
from jax import lax

D = 8192
HEADS = 64
KV_HEADS = 8
HEAD_DIM = 128
VOCAB = 32000
LEN = 2048
CAND = 4
REQS = 256


def rough_rows(key, shape):
    key_base, key_rough = jax.random.split(key, 2)
    width_all = shape[-1]
    normal_part = jnp.clip(jax.random.normal(key_base, shape, jnp.float32), -6.0, 6.0)
    ramp_scale = jnp.exp(math.log(3.0) * jnp.arange(width_all, dtype=jnp.float32) / width_all)
    rough_scale = jnp.exp(jax.random.uniform(key_rough, (width_all,), jnp.float32, 0.0, math.log(2.0)))
    values = normal_part * ramp_scale * rough_scale * 0.5
    return values


def query_columns(key, head_ids):
    column_key = jax.random.fold_in(key, 101)

    def one_head(head_id):
        head_key = jax.random.fold_in(column_key, head_id)
        return jnp.clip(jax.random.normal(head_key, (D, HEAD_DIM), jnp.float32), -6.0, 6.0) / math.sqrt(D)
    return jax.vmap(one_head)(head_ids)


def draw_w_query(key, part):
    columns = query_columns(key, jnp.arange(HEADS, dtype=jnp.int32))
    return jnp.transpose(columns, (1, 0, 2)).reshape(D, HEADS * HEAD_DIM).astype(jnp.bfloat16)


def draw_w_keyval(key, part):
    own_key = jax.random.fold_in(key, 37)
    key_pick, key_noise, key_value = jax.random.split(own_key, 3)
    group_size = HEADS // KV_HEADS
    picks = jax.random.randint(key_pick, (KV_HEADS,), 0, group_size, jnp.int32)
    head_ids = jnp.arange(KV_HEADS, dtype=jnp.int32) * group_size + picks
    aligned = query_columns(key, head_ids)
    aligned = jnp.transpose(aligned, (1, 0, 2)).reshape(D, KV_HEADS * HEAD_DIM)
    noise_part = jnp.clip(jax.random.normal(key_noise, (D, KV_HEADS * HEAD_DIM), jnp.float32), -6.0, 6.0) / math.sqrt(D)
    key_weight = 0.9 * aligned + 0.45 * noise_part
    value_weight = jnp.clip(jax.random.normal(key_value, (D, KV_HEADS * HEAD_DIM), jnp.float32), -6.0, 6.0) / math.sqrt(D)
    return jnp.stack([key_weight, value_weight], axis=0).astype(jnp.bfloat16)


def draw_w_output(key, part):
    key = jax.random.fold_in(key, 43)
    key_base, key_block = jax.random.split(key)
    rows_all = HEADS * HEAD_DIM
    normal_part = jnp.clip(jax.random.normal(key_base, (rows_all, D), jnp.float32), -6.0, 6.0) / math.sqrt(rows_all)
    heavy_block = jax.random.randint(key_block, (), 0, 4, jnp.int32)
    block_of_column = jnp.arange(D, dtype=jnp.int32) * 4 // D
    column_scale = jnp.where(block_of_column == heavy_block, 4.0, 1.0)
    return (normal_part * column_scale[None, :]).astype(jnp.bfloat16)


def draw_hidden_in(key, part):
    key = jax.random.fold_in(key, 11)
    key_cut = jax.random.fold_in(key, 41)
    values = rough_rows(key, (REQS, D))
    row_cut = jnp.where(jax.random.uniform(key_cut, (REQS, 1)) < 0.125, 1.0 / 16.0, 1.0)
    return (values * row_cut).astype(jnp.bfloat16)


def draw_premature(key, part):
    key = jax.random.fold_in(key, 23)
    return rough_rows(key, (CAND, REQS, D)).astype(jnp.bfloat16)


def draw_w_head(key, part):
    key = jax.random.fold_in(key, 13)
    key_base, key_column = jax.random.split(key, 2)
    normal_part = jnp.clip(jax.random.normal(key_base, (D, VOCAB), jnp.float32), -6.0, 6.0) / math.sqrt(D)
    column_scale = jnp.exp(jax.random.uniform(key_column, (VOCAB,), jnp.float32, 0.0, math.log(10.0)))
    column_scale = column_scale * jnp.exp(math.log(3.0) * jnp.arange(VOCAB, dtype=jnp.float32) / VOCAB)
    return (normal_part * column_scale).astype(jnp.bfloat16)


def draw_cache_keys(key, part):
    key = jax.random.fold_in(key, 17)
    key_base = jax.random.fold_in(key, 0)
    normal_part = jnp.clip(jax.random.normal(key_base, (REQS, LEN, KV_HEADS, HEAD_DIM), jnp.float32), -6.0, 6.0)
    values = normal_part
    return values.astype(jnp.bfloat16)


def draw_cache_lengths(key, part):
    key = jax.random.fold_in(key, 19)
    key_len, key_row = jax.random.split(key)
    lengths = jax.random.randint(key_len, (REQS,), LEN // 8, LEN, jnp.int32)
    chosen_row = jax.random.randint(key_row, (), 0, REQS, jnp.int32)
    return lengths.at[chosen_row].set(LEN - 1)


def set_ends(entries, key, least, high):
    index_at = [jax.random.randint(jax.random.fold_in(key, axis), (), 0, length) for axis, length in enumerate(entries.shape)]
    widest = entries.shape.index(max(entries.shape))
    neighbour = index_at[:widest] + [(index_at[widest] + 1) % entries.shape[widest]] + index_at[widest + 1:]
    return entries.at[tuple(index_at)].set(least).at[tuple(neighbour)].set(high)


def block_levels(rng, extent, pieces, low, largest):
    loudness = 1.0
    for dim, parts in pieces:
        steps = jax.random.uniform(jax.random.fold_in(jax.random.fold_in(rng, 6), dim), (parts,), jnp.float32, low / len(pieces), largest / len(pieces))
        loudness = loudness * jnp.repeat(jnp.exp(steps), extent[dim] // parts).reshape((-1,) + (1,) * (len(extent) - 1 - dim))
    return loudness


def scatter_about(rng, extent, width, reach, pieces=(), held_as=jnp.bfloat16):
    array = jax.random.normal(rng, extent, jnp.float32) * width
    if len(pieces) > 0:
        array = block_levels(rng, extent, pieces, -0.22, 0.18) * array
    return jnp.clip(array, min=-reach, max=reach).astype(held_as)


def setup_inputs(seed: int = 0) -> dict:
    splits = jax.random.split(jax.random.key(seed), 13)
    hidden_in = draw_hidden_in(jax.random.fold_in(splits[12], 71), 0)
    attn_gain = jnp.clip(1.0 + 0.15 * jax.random.normal(splits[1], (D,), jnp.float32), 0.25, 1.75)
    w_query = draw_w_query(jax.random.fold_in(splits[12], 71), 0)
    w_keyval = draw_w_keyval(jax.random.fold_in(splits[12], 71), 0)
    w_output = draw_w_output(jax.random.fold_in(splits[12], 71), 0)
    final_gain = jnp.clip(1.0 + 0.15 * jax.random.normal(splits[5], (D,), jnp.float32), 0.25, 1.75)
    w_head = draw_w_head(jax.random.fold_in(splits[12], 71), 0)
    cache_keys = draw_cache_keys(jax.random.fold_in(splits[12], 71), 0)
    cache_values = scatter_about(splits[8], (REQS, LEN, KV_HEADS, HEAD_DIM), 1.0, 6.0, ((0, 64), (2, 4)))
    cache_lengths = draw_cache_lengths(jax.random.fold_in(splits[12], 71), 0)
    premature = draw_premature(jax.random.fold_in(splits[12], 71), 0)
    premature_layer = set_ends(jax.random.randint(splits[11], (REQS,), 0, CAND), jax.random.fold_in(splits[11], 1), 0, CAND - 1).astype(jnp.int32)
    return {"hidden_in": hidden_in, "attn_gain": attn_gain, "w_query": w_query, "w_keyval": w_keyval, "w_output": w_output, "final_gain": final_gain, "w_head": w_head, "cache_keys": cache_keys, "cache_values": cache_values, "cache_lengths": cache_lengths, "premature": premature, "premature_layer": premature_layer}


EPSILON = 1e-05

def normalize(values, gain):
    return values * lax.rsqrt(lax.optimization_barrier(jnp.mean(values * values, axis=-1, keepdims=True)) + EPSILON) * gain

def rotate(heads, positions):
    half_dim = heads.shape[-1] // 2
    frequency = jnp.exp(-math.log(10000.0) * 2.0 * jnp.arange(half_dim, dtype=jnp.float32) / heads.shape[-1])
    angles = positions[:, None] * frequency[None, :]
    cos_part = jnp.cos(angles)[:, None, :]
    sin_part = jnp.sin(angles)[:, None, :]
    lower_half = heads[..., :half_dim]
    upper_half = heads[..., half_dim:]
    return jnp.concatenate([lower_half * cos_part - upper_half * sin_part, upper_half * cos_part + lower_half * sin_part], axis=-1)

def attend_one(operands):
    query_row, keys_cache, values_cache, key_row, value_row, length = operands
    group_size = HEADS // KV_HEADS
    grouped = query_row.reshape(KV_HEADS, group_size, HEAD_DIM).astype(jnp.float32)
    scores = jnp.einsum('kgd,lkd->kgl', grouped, keys_cache.astype(jnp.float32)) / math.sqrt(HEAD_DIM)
    own_score = jnp.einsum('kgd,kd->kg', grouped, key_row.astype(jnp.float32)) / math.sqrt(HEAD_DIM)
    valid_mask = jnp.arange(LEN) < length
    scores = jnp.where(valid_mask[None, None, :], scores, -jnp.inf)
    row_peak = jnp.maximum(lax.optimization_barrier(jnp.max(scores, axis=-1)), own_score)
    expo = jnp.exp(scores - row_peak[..., None])
    own_expo = jnp.exp(own_score - row_peak)
    sum_exp = lax.optimization_barrier(jnp.sum(expo, axis=-1)) + own_expo
    weights = (expo / sum_exp[..., None]).astype(jnp.bfloat16)
    own_weight = (own_expo / sum_exp).astype(jnp.bfloat16)
    mixed = jnp.einsum('kgl,lkd->kgd', weights.astype(jnp.float32), values_cache.astype(jnp.float32))
    mixed = mixed + own_weight.astype(jnp.float32)[..., None] * value_row.astype(jnp.float32)[:, None, :]
    return mixed.reshape(HEADS * HEAD_DIM).astype(jnp.bfloat16)

def reference(hidden_in, attn_gain, w_query, w_keyval, w_output, final_gain, w_head, cache_keys, cache_values, cache_lengths, premature, premature_layer):
    hidden = hidden_in.astype(jnp.float32)
    normed = normalize(hidden, attn_gain).astype(jnp.bfloat16)
    queries = jnp.dot(normed, w_query, preferred_element_type=jnp.float32).reshape(REQS, HEADS, HEAD_DIM)
    keys_new = jnp.dot(normed, w_keyval[0], preferred_element_type=jnp.float32).reshape(REQS, KV_HEADS, HEAD_DIM)
    values_new = jnp.dot(normed, w_keyval[1], preferred_element_type=jnp.float32).reshape(REQS, KV_HEADS, HEAD_DIM)
    positions = cache_lengths.astype(jnp.float32)
    rot_queries = rotate(queries, positions).astype(jnp.bfloat16)
    rot_keys = rotate(keys_new, positions).astype(jnp.bfloat16)
    values_new = values_new.astype(jnp.bfloat16)
    attended = lax.map(attend_one, (rot_queries, cache_keys, cache_values, rot_keys, values_new, cache_lengths))
    residual = hidden + jnp.dot(attended, w_output, preferred_element_type=jnp.float32)
    final_rows = normalize(residual, final_gain).astype(jnp.bfloat16)
    chosen = premature_layer[None, :] == jnp.arange(CAND, dtype=jnp.int32)[:, None]
    early_full = lax.optimization_barrier(jnp.sum(jnp.where(chosen[:, :, None], premature.astype(jnp.float32), jnp.float32(0.0)), axis=0))
    early_rows = normalize(early_full, final_gain).astype(jnp.bfloat16)
    final_logits = jnp.dot(final_rows, w_head, preferred_element_type=jnp.float32)
    early_logits = jnp.dot(early_rows, w_head, preferred_element_type=jnp.float32)
    return jax.nn.log_softmax(final_logits, axis=-1) - jax.nn.log_softmax(early_logits, axis=-1)
```

```python
import math

import jax
import jax.numpy as jnp
from jax import lax
from jax.experimental import pallas as pl
from jax.experimental.pallas import tpu as pltpu
from jax.sharding import Mesh
from jax.sharding import PartitionSpec as P

HEAD_DIM = 128
EPSILON = 1e-05
PLANE = ("x", "z", "c")
CHIPS = ("x", "z")
NX, NZ, NC, NT = 4, 8, 2, 4
BF = jnp.bfloat16
F32 = jnp.float32


def normalize(values, gain):
    return values * lax.rsqrt(jnp.mean(values * values, axis=-1, keepdims=True) + EPSILON) * gain


def rotate(heads, positions):
    half_dim = heads.shape[-1] // 2
    frequency = jnp.exp(
        -math.log(10000.0) * 2.0 * jnp.arange(half_dim, dtype=jnp.float32) / heads.shape[-1]
    )
    angles = positions[:, None] * frequency[None, :]
    cos_part = jnp.cos(angles)[:, None, :]
    sin_part = jnp.sin(angles)[:, None, :]
    lower_half = heads[..., :half_dim]
    upper_half = heads[..., half_dim:]
    return jnp.concatenate(
        [
            lower_half * cos_part - upper_half * sin_part,
            upper_half * cos_part + lower_half * sin_part,
        ],
        axis=-1,
    )


def swap_cores(values):
    return lax.ppermute(values, "c", [(0, 1), (1, 0)])


def exchange(values, axes):
    return lax.all_to_all(values, axes, 0, 0, tiled=True)


def by_core(own, other):
    first = lax.axis_index("c") == 0
    return jnp.where(first, own, other), jnp.where(first, other, own)


def in_rows(ref, chips):
    return jnp.concatenate([ref[chip].astype(F32) for chip in chips], axis=0)


def natural_rows(own, other, first, req_dev):
    core_0, core_1 = jnp.where(first, own, other), jnp.where(first, other, own)
    ordered = []
    for z in range(NZ):
        span = slice(z * req_dev, (z + 1) * req_dev)
        ordered += [core_0[span], core_1[span]]
    return jnp.concatenate(ordered, axis=0)


def early_head_kernel(core_ref, own_ref, other_ref, w_ref, out_ref, acc_ref):
    step = pl.program_id(0)

    @pl.when(step == 0)
    def _():
        acc_ref[...] = jnp.zeros_like(acc_ref)

    chips = range(NX * NZ)
    rows = jnp.concatenate([in_rows(own_ref.at[0], chips), in_rows(other_ref.at[0], chips)], axis=0)
    acc_ref[...] += lax.dot_general(
        rows.astype(BF), w_ref[...], (((1,), (1,)), ((), ())), preferred_element_type=F32
    )

    @pl.when(step == pl.num_programs(0) - 1)
    def _():
        req_dev = own_ref.shape[2]
        half = NZ * req_dev
        for x in range(NX):
            own = acc_ref[x * half : (x + 1) * half]
            other = acc_ref[(NX + x) * half : (NX + x + 1) * half]
            out_ref[x] = natural_rows(own, other, core_ref[0] == 0, req_dev)


def early_head(core, own, other, w_head_t):
    quarters, chips, req_dev, width = own.shape
    vocab_dev = w_head_t.shape[0]
    rows = pl.BlockSpec((1, chips, req_dev, width), lambda q: (q, 0, 0, 0))
    group = NZ * NC * req_dev
    return pl.pallas_call(
        early_head_kernel,
        grid=(quarters,),
        out_shape=jax.ShapeDtypeStruct((NX, group, vocab_dev), F32),
        in_specs=[
            pl.BlockSpec(memory_space=pltpu.SMEM),
            rows,
            rows,
            pl.BlockSpec((vocab_dev, width), lambda q: (0, q)),
        ],
        out_specs=pl.BlockSpec((NX, group, vocab_dev), lambda q: (0, 0, 0)),
        scratch_shapes=[pltpu.VMEM((NX * group, vocab_dev), F32)],
        compiler_params=pltpu.CompilerParams(vmem_limit_bytes=24 * 2**20),
        cost_estimate=pl.CostEstimate(
            flops=2 * NX * group * vocab_dev * width * quarters,
            bytes_accessed=2 * vocab_dev * width * quarters,
            transcendentals=0,
        ),
        name="early",
    )(core, own, other, w_head_t)


def project_kernel(core_ref, own_ref, other_ref, w_ref, out_ref):
    req_dev = own_ref.shape[1]
    pieces = [ref[z].astype(F32) for ref in (own_ref, other_ref) for z in range(NZ)]
    rows = jnp.concatenate(pieces, axis=0).astype(BF)
    total = jnp.dot(rows, w_ref[...], preferred_element_type=F32)
    half = total.shape[0] // 2
    first = core_ref[0] == 0
    own, other = total[:half], total[half:]
    core_0, core_1 = jnp.where(first, own, other), jnp.where(first, other, own)
    ordered = []
    for z in range(NZ):
        span = slice(z * req_dev, (z + 1) * req_dev)
        ordered += [core_0[span], core_1[span]]
    out_ref[0] = jnp.concatenate(ordered, axis=0)


def project(core, own, other, w_output):
    _, req_dev, width = own.shape
    cols = w_output.shape[1]
    group = NZ * NC * req_dev
    rows = pl.BlockSpec((NZ, req_dev, width), lambda x: (x, 0, 0))
    return pl.pallas_call(
        project_kernel,
        grid=(NX,),
        out_shape=jax.ShapeDtypeStruct((NX, group, cols), F32),
        in_specs=[
            pl.BlockSpec(memory_space=pltpu.SMEM),
            rows,
            rows,
            pl.BlockSpec((width, cols), lambda x: (0, 0)),
        ],
        out_specs=pl.BlockSpec((1, group, cols), lambda x: (x, 0, 0)),
        compiler_params=pltpu.CompilerParams(vmem_limit_bytes=24 * 2**20),
        cost_estimate=pl.CostEstimate(
            flops=2 * NX * group * cols * width,
            bytes_accessed=4 * NX * group * width,
            transcendentals=0,
        ),
        name="project",
    )(core, own, other, w_output)


def settle_kernel(block_ref, parts_ref, hidden_ref, gain_ref, out_ref):
    residual = jnp.sum(parts_ref[...], axis=0) + hidden_ref[...].astype(F32)
    scaled = (residual * gain_ref[pl.ds(block_ref[0], 1), :]).astype(BF)
    out_ref[...] = jnp.broadcast_to(scaled[None], out_ref.shape)


def settle(block, parts, hidden_rows, final_gain):
    group, cols = hidden_rows.shape
    vmem = pl.BlockSpec(memory_space=pltpu.VMEM)
    return pl.pallas_call(
        settle_kernel,
        out_shape=jax.ShapeDtypeStruct((NX * NZ, group, cols), BF),
        in_specs=[pl.BlockSpec(memory_space=pltpu.SMEM), vmem, vmem, vmem],
        out_specs=vmem,
        compiler_params=pltpu.CompilerParams(vmem_limit_bytes=16 * 2**20),
        name="settle",
    )(block, parts, hidden_rows, final_gain.reshape(-1, cols))


def opening_kernel(
    layer_ref, hidden_ref, attn_gain_ref, final_gain_ref, premature_ref, out_ref, early_ref
):
    hidden = hidden_ref[...].astype(F32)
    normed = normalize(hidden, attn_gain_ref[...])
    joined = jnp.concatenate([normed, hidden], axis=0).astype(BF)
    cols = out_ref.shape[2]
    for block in range(out_ref.shape[0]):
        out_ref[block] = joined[:, block * cols : (block + 1) * cols]
    rows = []
    for row in range(hidden.shape[0]):
        rows.append(premature_ref[layer_ref[row], pl.ds(row, 1), :].astype(F32))
    early = normalize(jnp.concatenate(rows, axis=0), final_gain_ref[...])
    early_ref[...] = early.astype(BF)


def opening_blocks(hidden_in, attn_gain, final_gain, premature, premature_layer):
    req_dev, width_all = hidden_in.shape
    chips = NX * NZ
    vmem = pl.BlockSpec(memory_space=pltpu.VMEM)
    return pl.pallas_call(
        opening_kernel,
        out_shape=(
            jax.ShapeDtypeStruct((chips, 2 * req_dev, width_all // chips), BF),
            jax.ShapeDtypeStruct((req_dev, width_all), BF),
        ),
        in_specs=[pl.BlockSpec(memory_space=pltpu.SMEM), vmem, vmem, vmem, vmem],
        out_specs=(vmem, vmem),
        compiler_params=pltpu.CompilerParams(vmem_limit_bytes=16 * 2**20),
        name="opening",
    )(premature_layer, hidden_in, attn_gain[None], final_gain[None], premature)


def head_kernel(
    core_ref, own_ref, other_ref, gain_ref, *refs
):
    *early_refs, w_hbm_ref, diff_ref, stats_ref, w_ref, arrived = refs
    chips, group, cols = own_ref.shape
    first = core_ref[0] == 0
    pair = NC * cols
    per_copy = chips // arrived.shape[0]
    copies = []
    for k in range(arrived.shape[0]):
        span = pl.ds(k * per_copy * pair, per_copy * pair)
        copies.append(
            pltpu.make_async_copy(w_hbm_ref.at[:, span], w_ref.at[:, span], arrived.at[k])
        )
        copies[-1].start()
    total = None
    squares = jnp.zeros((group, pair), F32)
    for chip in range(chips):
        if chip % per_copy == 0:
            copies[chip // per_copy].wait()
        own, other = own_ref[chip], other_ref[chip]
        final_pair = jnp.concatenate(
            [jnp.where(first, own, other), jnp.where(first, other, own)], axis=1
        )
        gains = [gain_ref[NC * chip + k : NC * chip + k + 1, :] for k in range(NC)]
        unscaled = final_pair.astype(F32) / jnp.concatenate(gains, axis=1)
        squares = squares + unscaled * unscaled
        term = lax.dot_general(
            final_pair,
            w_ref[:, chip * pair : (chip + 1) * pair],
            (((1,), (1,)), ((), ())),
            preferred_element_type=F32,
        )
        total = term if total is None else total + term
    mean = jnp.sum(squares, axis=1, keepdims=True) / (chips * pair)
    final = total * lax.rsqrt(mean + EPSILON)
    early = early_refs[0][...]
    for early_ref in early_refs[1:]:
        early = early + early_ref[...]
    peaks, sums = [], []
    for logits in (final, early):
        peak = jnp.max(logits, axis=1, keepdims=True)
        peaks.append(peak)
        sums.append(jnp.sum(jnp.exp(logits - peak), axis=1, keepdims=True))
    square = (2 * group, 2 * group)
    lines = [
        jnp.broadcast_to(jnp.concatenate(parts, axis=0), square).T[:1] for parts in (peaks, sums)
    ]
    stats_ref[...] = jnp.broadcast_to(jnp.concatenate(lines, axis=0)[None], stats_ref.shape)
    diff_ref[...] = final - early


def head(core, own, other, gain, early, w_head_t):
    _, group, cols = own.shape
    vocab_dev, width_all = w_head_t.shape
    plane_size = NX * NZ * NC
    vmem = pl.BlockSpec(memory_space=pltpu.VMEM)
    return pl.pallas_call(
        head_kernel,
        out_shape=(
            jax.ShapeDtypeStruct((group, vocab_dev), F32),
            jax.ShapeDtypeStruct((plane_size, 2, 2 * group), F32),
        ),
        in_specs=[pl.BlockSpec(memory_space=pltpu.SMEM)]
        + [vmem] * (3 + len(early))
        + [pl.BlockSpec(memory_space=pl.ANY)],
        out_specs=(vmem, vmem),
        scratch_shapes=[pltpu.VMEM((vocab_dev, width_all), BF), pltpu.SemaphoreType.DMA((8,))],
        compiler_params=pltpu.CompilerParams(vmem_limit_bytes=56 * 2**20),
        cost_estimate=pl.CostEstimate(
            flops=2 * group * vocab_dev * width_all,
            bytes_accessed=2 * vocab_dev * width_all,
            transcendentals=2 * group * vocab_dev,
        ),
        name="head",
    )(core, own, other, gain, *early, w_head_t)


def finish_kernel(stats_ref, diff_ref, out_ref):
    group = diff_ref.shape[0]
    peaks = stats_ref[:, 0, :]
    peak = jnp.max(peaks, axis=0, keepdims=True)
    total = jnp.sum(stats_ref[:, 1, :] * jnp.exp(peaks - peak), axis=0, keepdims=True)
    log_total = peak + jnp.log(total)
    offset = log_total[:, :group] - log_total[:, group:]
    offset = jnp.broadcast_to(offset, (group, group)).T[:, :1]
    out_ref[...] = diff_ref[...] - offset


def finish(stats, diff):
    vmem = pl.BlockSpec(memory_space=pltpu.VMEM)
    return pl.pallas_call(
        finish_kernel,
        out_shape=jax.ShapeDtypeStruct(diff.shape, F32),
        in_specs=[vmem, vmem],
        out_specs=vmem,
        compiler_params=pltpu.CompilerParams(vmem_limit_bytes=8 * 2**20),
        name="finish",
    )(stats, diff)


def attend(rot_queries, rot_keys, values_new, cache_keys, cache_values, cache_lengths):
    req_dev, slot_count, kv_dev, _ = cache_keys.shape
    group_size = rot_queries.shape[1] // kv_dev
    grouped = rot_queries.reshape(req_dev, kv_dev, group_size, HEAD_DIM)
    scores = jnp.einsum(
        "nkgd,nlkd->nkgl", grouped, cache_keys, preferred_element_type=jnp.float32
    ) / math.sqrt(HEAD_DIM)
    own_score = jnp.einsum(
        "nkgd,nkd->nkg", grouped, rot_keys, preferred_element_type=jnp.float32
    ) / math.sqrt(HEAD_DIM)
    valid_mask = jnp.arange(slot_count)[None, :] < cache_lengths[:, None]
    scores = jnp.where(valid_mask[:, None, None, :], scores, -jnp.inf)
    row_peak = jnp.maximum(jnp.max(scores, axis=-1), own_score)
    expo = jnp.exp(scores - row_peak[..., None])
    own_expo = jnp.exp(own_score - row_peak)
    sum_exp = jnp.sum(expo, axis=-1) + own_expo
    weights = (expo / sum_exp[..., None]).astype(BF)
    own_weight = (own_expo / sum_exp).astype(BF)
    mixed = jnp.einsum("nkgl,nlkd->nkgd", weights, cache_values, preferred_element_type=jnp.float32)
    mixed = mixed + own_weight.astype(F32)[..., None] * values_new.astype(F32)[:, :, None, :]
    return mixed.reshape(req_dev, kv_dev * group_size * HEAD_DIM).astype(BF)


def shards(
    hidden_in,
    attn_gain,
    w_query,
    w_keyval,
    w_output,
    final_gain,
    w_head,
    cache_keys,
    cache_values,
    cache_lengths,
    premature,
    premature_layer,
):
    req_dev, width_all = hidden_in.shape
    plane_size = NX * NZ * NC
    t_pos = lax.axis_index("t")
    c_pos = lax.axis_index("c")
    plane_pos = lax.axis_index(PLANE)
    cols = width_all // plane_size

    head_t = lax.all_gather(w_head, "t", axis=0, tiled=True).T

    both, early_rows = opening_blocks(
        hidden_in, attn_gain, final_gain, premature, premature_layer
    )
    q_both = jnp.concatenate(by_core(w_query, swap_cores(w_query)), axis=0)
    kv_both = jnp.concatenate(by_core(w_keyval, swap_cores(w_keyval)), axis=1)
    w_both = jnp.concatenate([q_both, kv_both[0], kv_both[1]], axis=1)
    both, w_both = lax.optimization_barrier((exchange(both, CHIPS), w_both))
    group = NZ * NC * req_dev
    normed = both[:, :req_dev].reshape(NX * NZ * req_dev, NC * cols)
    hidden_rows = both[:, req_dev:].reshape(NX, NZ, req_dev, NC, cols)
    hidden_rows = lax.dynamic_index_in_dim(hidden_rows, t_pos, 0, keepdims=False)
    hidden_own = lax.dynamic_index_in_dim(hidden_rows, c_pos, 2, keepdims=False)
    hidden_sent = lax.dynamic_index_in_dim(hidden_rows, 1 - c_pos, 2, keepdims=False)
    hidden_rows = jnp.stack(by_core(hidden_own, swap_cores(hidden_sent)), axis=1)
    hidden_rows = hidden_rows.reshape(group, cols)

    slice_width = width_all // NT
    early_part = lax.dynamic_slice_in_dim(early_rows, t_pos * slice_width, slice_width, 1)
    early_part = early_part.reshape(req_dev, NX, slice_width // NX).transpose(1, 0, 2)
    early_quarters = jnp.broadcast_to(early_part[:, None], (NX, NZ) + early_part.shape[1:])
    early_quarters = early_quarters.reshape(NX * NZ, req_dev, slice_width // NX)

    sums = jnp.dot(normed, w_both, preferred_element_type=F32)
    blocks = sums.astype(BF).reshape(NX * NZ, req_dev, w_both.shape[1])
    summed = exchange(jnp.concatenate([blocks, early_quarters], axis=2), CHIPS)
    projected = jnp.sum(summed[:, :, : w_both.shape[1]].astype(F32), axis=0)
    early = lax.all_gather(summed[:, :, w_both.shape[1] :], "x", axis=0)

    query_cols = w_query.shape[1]
    pair_cols = w_keyval.shape[2]
    heads_dev = query_cols // HEAD_DIM
    kv_dev = pair_cols // HEAD_DIM
    queries = projected[:, :query_cols].reshape(req_dev, heads_dev, HEAD_DIM)
    keys_new = projected[:, query_cols : query_cols + pair_cols].reshape(req_dev, kv_dev, HEAD_DIM)
    values_new = (
        projected[:, query_cols + pair_cols :].reshape(req_dev, kv_dev, HEAD_DIM).astype(BF)
    )
    positions = cache_lengths.astype(F32)
    rot_queries = rotate(queries, positions).astype(BF)
    rot_keys = rotate(keys_new, positions).astype(BF)
    attended = attend(rot_queries, rot_keys, values_new, cache_keys, cache_values, cache_lengths)

    own_rows = exchange(jnp.broadcast_to(attended[None], (NX * NZ,) + attended.shape), CHIPS)
    own_rows, early = lax.optimization_barrier((own_rows, early))
    other_rows = swap_cores(own_rows)
    parts = project(c_pos[None], own_rows, other_rows, w_output)
    parts, early = lax.optimization_barrier((parts, early))
    parts = exchange(parts, ("t",))

    early_sums = early_head(c_pos[None], early, swap_cores(early), w_head.T)
    parts, early_sums = lax.optimization_barrier((parts, early_sums))
    early_parts = []
    for k in range(NT):
        block = lax.dynamic_index_in_dim(early_sums, (t_pos + k) % NT, 0, keepdims=False)
        if k > 0:
            block = lax.ppermute(block, "t", [(t, (t + k) % NT) for t in range(NT)])
        early_parts.append(block)

    scaled = settle(plane_pos[None], parts, hidden_rows, final_gain)
    own_cols = exchange(scaled, CHIPS)
    own_cols, *early_parts = lax.optimization_barrier((own_cols, *early_parts))
    other_cols = swap_cores(own_cols)
    gain = final_gain.reshape(plane_size, cols)
    diff, stats = head(c_pos[None], own_cols, other_cols, gain, early_parts, head_t)

    stats = exchange(stats, PLANE)
    return finish(stats, diff)


def solution(mesh):
    fine = Mesh(mesh.devices.reshape(NT, NX, NZ, NC), ("t", "x", "z", "c"))
    placed = (
        P(PLANE, None),
        P(),
        P(PLANE, "t"),
        P(None, PLANE, "t"),
        P("t", PLANE),
        P(),
        P("t", PLANE),
        P(PLANE, None, "t", None),
        P(PLANE, None, "t", None),
        P(PLANE),
        P(None, PLANE, None),
        P(PLANE),
    )
    return jax.shard_map(
        shards, mesh=fine, in_specs=placed, out_specs=P("t", PLANE), check_vma=False
    )
```

```python
import math

import jax
import jax.numpy as jnp
from jax import lax
from jax.experimental import pallas as pl
from jax.experimental.pallas import tpu as pltpu
from jax.sharding import Mesh
from jax.sharding import PartitionSpec as P

HEAD_DIM = 128
EPSILON = 1e-05
PLANE = ("x", "z", "c")
CHIPS = ("x", "z")
NX, NZ, NC, NT = 4, 8, 2, 4
BF = jnp.bfloat16
F32 = jnp.float32


def normalize(values, gain):
    return values * lax.rsqrt(jnp.mean(values * values, axis=-1, keepdims=True) + EPSILON) * gain


def rotate(heads, positions):
    half_dim = heads.shape[-1] // 2
    frequency = jnp.exp(
        -math.log(10000.0) * 2.0 * jnp.arange(half_dim, dtype=jnp.float32) / heads.shape[-1]
    )
    angles = positions[:, None] * frequency[None, :]
    cos_part = jnp.cos(angles)[:, None, :]
    sin_part = jnp.sin(angles)[:, None, :]
    lower_half = heads[..., :half_dim]
    upper_half = heads[..., half_dim:]
    return jnp.concatenate(
        [
            lower_half * cos_part - upper_half * sin_part,
            upper_half * cos_part + lower_half * sin_part,
        ],
        axis=-1,
    )


def swap_cores(values):
    return lax.ppermute(values, "c", [(0, 1), (1, 0)])


def exchange(values, axes):
    return lax.all_to_all(values, axes, 0, 0, tiled=True)


def by_core(own, other):
    first = lax.axis_index("c") == 0
    return jnp.where(first, own, other), jnp.where(first, other, own)


def in_rows(ref, chips):
    return jnp.concatenate([ref[chip].astype(F32) for chip in chips], axis=0)


def natural_rows(own, other, first, req_dev):
    core_0, core_1 = jnp.where(first, own, other), jnp.where(first, other, own)
    ordered = []
    for z in range(NZ):
        span = slice(z * req_dev, (z + 1) * req_dev)
        ordered += [core_0[span], core_1[span]]
    return jnp.concatenate(ordered, axis=0)


def early_head_kernel(core_ref, own_ref, other_ref, w_ref, out_ref, acc_ref):
    step = pl.program_id(0)

    @pl.when(step == 0)
    def _():
        acc_ref[...] = jnp.zeros_like(acc_ref)

    chips = range(NX * NZ)
    rows = jnp.concatenate([in_rows(own_ref.at[0], chips), in_rows(other_ref.at[0], chips)], axis=0)
    acc_ref[...] += lax.dot_general(
        rows.astype(BF), w_ref[...], (((1,), (1,)), ((), ())), preferred_element_type=F32
    )

    @pl.when(step == pl.num_programs(0) - 1)
    def _():
        req_dev = own_ref.shape[2]
        half = NZ * req_dev
        for x in range(NX):
            own = acc_ref[x * half : (x + 1) * half]
            other = acc_ref[(NX + x) * half : (NX + x + 1) * half]
            out_ref[x] = natural_rows(own, other, core_ref[0] == 0, req_dev)


def early_head(core, own, other, w_head_t):
    quarters, chips, req_dev, width = own.shape
    vocab_dev = w_head_t.shape[0]
    rows = pl.BlockSpec((1, chips, req_dev, width), lambda q: (q, 0, 0, 0))
    group = NZ * NC * req_dev
    return pl.pallas_call(
        early_head_kernel,
        grid=(quarters,),
        out_shape=jax.ShapeDtypeStruct((NX, group, vocab_dev), F32),
        in_specs=[
            pl.BlockSpec(memory_space=pltpu.SMEM),
            rows,
            rows,
            pl.BlockSpec((vocab_dev, width), lambda q: (0, q)),
        ],
        out_specs=pl.BlockSpec((NX, group, vocab_dev), lambda q: (0, 0, 0)),
        scratch_shapes=[pltpu.VMEM((NX * group, vocab_dev), F32)],
        compiler_params=pltpu.CompilerParams(vmem_limit_bytes=24 * 2**20),
        cost_estimate=pl.CostEstimate(
            flops=2 * NX * group * vocab_dev * width * quarters,
            bytes_accessed=2 * vocab_dev * width * quarters,
            transcendentals=0,
        ),
        name="early",
    )(core, own, other, w_head_t)


def project_kernel(core_ref, own_ref, other_ref, w_ref, out_ref):
    req_dev = own_ref.shape[1]
    pieces = [ref[z].astype(F32) for ref in (own_ref, other_ref) for z in range(NZ)]
    rows = jnp.concatenate(pieces, axis=0).astype(BF)
    total = jnp.dot(rows, w_ref[...], preferred_element_type=F32)
    half = total.shape[0] // 2
    first = core_ref[0] == 0
    own, other = total[:half], total[half:]
    core_0, core_1 = jnp.where(first, own, other), jnp.where(first, other, own)
    ordered = []
    for z in range(NZ):
        span = slice(z * req_dev, (z + 1) * req_dev)
        ordered += [core_0[span], core_1[span]]
    out_ref[0] = jnp.concatenate(ordered, axis=0)


def project(core, own, other, w_output):
    _, req_dev, width = own.shape
    cols = w_output.shape[1]
    group = NZ * NC * req_dev
    rows = pl.BlockSpec((NZ, req_dev, width), lambda x: (x, 0, 0))
    return pl.pallas_call(
        project_kernel,
        grid=(NX,),
        out_shape=jax.ShapeDtypeStruct((NX, group, cols), F32),
        in_specs=[
            pl.BlockSpec(memory_space=pltpu.SMEM),
            rows,
            rows,
            pl.BlockSpec((width, cols), lambda x: (0, 0)),
        ],
        out_specs=pl.BlockSpec((1, group, cols), lambda x: (x, 0, 0)),
        compiler_params=pltpu.CompilerParams(vmem_limit_bytes=24 * 2**20),
        cost_estimate=pl.CostEstimate(
            flops=2 * NX * group * cols * width,
            bytes_accessed=4 * NX * group * width,
            transcendentals=0,
        ),
        name="project",
    )(core, own, other, w_output)


def settle_kernel(block_ref, parts_ref, hidden_ref, gain_ref, out_ref):
    residual = jnp.sum(parts_ref[...], axis=0) + hidden_ref[...].astype(F32)
    scaled = (residual * gain_ref[pl.ds(block_ref[0], 1), :]).astype(BF)
    out_ref[...] = jnp.broadcast_to(scaled[None], out_ref.shape)


def settle(block, parts, hidden_rows, final_gain):
    group, cols = hidden_rows.shape
    vmem = pl.BlockSpec(memory_space=pltpu.VMEM)
    return pl.pallas_call(
        settle_kernel,
        out_shape=jax.ShapeDtypeStruct((NX * NZ, group, cols), BF),
        in_specs=[pl.BlockSpec(memory_space=pltpu.SMEM), vmem, vmem, vmem],
        out_specs=vmem,
        compiler_params=pltpu.CompilerParams(vmem_limit_bytes=16 * 2**20),
        name="settle",
    )(block, parts, hidden_rows, final_gain.reshape(-1, cols))


def opening_kernel(
    layer_hbm, hidden_hbm, attn_gain_hbm, final_gain_hbm, premature_hbm, out_ref, early_ref,
    layer_ref, hidden_ref, attn_gain_ref, final_gain_ref, premature_ref, arrived,
):
    pairs = [
        (hidden_hbm, hidden_ref),
        (attn_gain_hbm, attn_gain_ref),
        (premature_hbm, premature_ref),
        (final_gain_hbm, final_gain_ref),
        (layer_hbm, layer_ref),
    ]
    copies = []
    for k, (source, target) in enumerate(pairs):
        copies.append(pltpu.make_async_copy(source, target, arrived.at[k]))
        copies[-1].start()
    copies[0].wait()
    copies[1].wait()
    hidden = hidden_ref[...].astype(F32)
    normed = normalize(hidden, attn_gain_ref[...])
    joined = jnp.concatenate([normed, hidden], axis=0).astype(BF)
    cols = out_ref.shape[2]
    for block in range(out_ref.shape[0]):
        out_ref[block] = joined[:, block * cols : (block + 1) * cols]
    for copy in copies[2:]:
        copy.wait()
    rows = []
    for row in range(hidden.shape[0]):
        rows.append(premature_ref[layer_ref[row], pl.ds(row, 1), :].astype(F32))
    early = normalize(jnp.concatenate(rows, axis=0), final_gain_ref[...])
    early_ref[...] = early.astype(BF)


def opening_blocks(hidden_in, attn_gain, final_gain, premature, premature_layer):
    req_dev, width_all = hidden_in.shape
    chips = NX * NZ
    vmem = pl.BlockSpec(memory_space=pltpu.VMEM)
    return pl.pallas_call(
        opening_kernel,
        out_shape=(
            jax.ShapeDtypeStruct((chips, 2 * req_dev, width_all // chips), BF),
            jax.ShapeDtypeStruct((req_dev, width_all), BF),
        ),
        in_specs=[pl.BlockSpec(memory_space=pl.ANY)] * 5,
        out_specs=(vmem, vmem),
        scratch_shapes=[
            pltpu.SMEM(premature_layer.shape, premature_layer.dtype),
            pltpu.VMEM(hidden_in.shape, hidden_in.dtype),
            pltpu.VMEM((1, width_all), F32),
            pltpu.VMEM((1, width_all), F32),
            pltpu.VMEM(premature.shape, premature.dtype),
            pltpu.SemaphoreType.DMA((5,)),
        ],
        compiler_params=pltpu.CompilerParams(vmem_limit_bytes=60 * 2**20),
        name="opening",
    )(premature_layer, hidden_in, attn_gain[None], final_gain[None], premature)


def head_kernel(
    core_ref, own_ref, other_ref, gain_ref, *refs
):
    *early_refs, w_hbm_ref, diff_ref, stats_ref, w_ref, arrived = refs
    chips, group, cols = own_ref.shape
    first = core_ref[0] == 0
    pair = NC * cols
    per_copy = chips // arrived.shape[0]
    copies = []
    for k in range(arrived.shape[0]):
        span = pl.ds(k * per_copy * pair, per_copy * pair)
        copies.append(
            pltpu.make_async_copy(w_hbm_ref.at[:, span], w_ref.at[:, span], arrived.at[k])
        )
        copies[-1].start()
    total = None
    squares = jnp.zeros((group, pair), F32)
    for chip in range(chips):
        if chip % per_copy == 0:
            copies[chip // per_copy].wait()
        own, other = own_ref[chip], other_ref[chip]
        final_pair = jnp.concatenate(
            [jnp.where(first, own, other), jnp.where(first, other, own)], axis=1
        )
        gains = [gain_ref[NC * chip + k : NC * chip + k + 1, :] for k in range(NC)]
        unscaled = final_pair.astype(F32) / jnp.concatenate(gains, axis=1)
        squares = squares + unscaled * unscaled
        term = lax.dot_general(
            final_pair,
            w_ref[:, chip * pair : (chip + 1) * pair],
            (((1,), (1,)), ((), ())),
            preferred_element_type=F32,
        )
        total = term if total is None else total + term
    mean = jnp.sum(squares, axis=1, keepdims=True) / (chips * pair)
    final = total * lax.rsqrt(mean + EPSILON)
    early = early_refs[0][...]
    for early_ref in early_refs[1:]:
        early = early + early_ref[...]
    peaks, sums = [], []
    for logits in (final, early):
        peak = jnp.max(logits, axis=1, keepdims=True)
        peaks.append(peak)
        sums.append(jnp.sum(jnp.exp(logits - peak), axis=1, keepdims=True))
    square = (2 * group, 2 * group)
    lines = [
        jnp.broadcast_to(jnp.concatenate(parts, axis=0), square).T[:1] for parts in (peaks, sums)
    ]
    stats_ref[...] = jnp.broadcast_to(jnp.concatenate(lines, axis=0)[None], stats_ref.shape)
    diff_ref[...] = final - early


def head(core, own, other, gain, early, w_head_t):
    _, group, cols = own.shape
    vocab_dev, width_all = w_head_t.shape
    plane_size = NX * NZ * NC
    vmem = pl.BlockSpec(memory_space=pltpu.VMEM)
    return pl.pallas_call(
        head_kernel,
        out_shape=(
            jax.ShapeDtypeStruct((group, vocab_dev), F32),
            jax.ShapeDtypeStruct((plane_size, 2, 2 * group), F32),
        ),
        in_specs=[pl.BlockSpec(memory_space=pltpu.SMEM)]
        + [vmem] * (3 + len(early))
        + [pl.BlockSpec(memory_space=pl.ANY)],
        out_specs=(vmem, vmem),
        scratch_shapes=[pltpu.VMEM((vocab_dev, width_all), BF), pltpu.SemaphoreType.DMA((8,))],
        compiler_params=pltpu.CompilerParams(vmem_limit_bytes=56 * 2**20),
        cost_estimate=pl.CostEstimate(
            flops=2 * group * vocab_dev * width_all,
            bytes_accessed=2 * vocab_dev * width_all,
            transcendentals=2 * group * vocab_dev,
        ),
        name="head",
    )(core, own, other, gain, *early, w_head_t)


def finish_kernel(stats_ref, diff_ref, out_ref):
    group = diff_ref.shape[0]
    peaks = stats_ref[:, 0, :]
    peak = jnp.max(peaks, axis=0, keepdims=True)
    total = jnp.sum(stats_ref[:, 1, :] * jnp.exp(peaks - peak), axis=0, keepdims=True)
    log_total = peak + jnp.log(total)
    offset = log_total[:, :group] - log_total[:, group:]
    offset = jnp.broadcast_to(offset, (group, group)).T[:, :1]
    out_ref[...] = diff_ref[...] - offset


def finish(stats, diff):
    vmem = pl.BlockSpec(memory_space=pltpu.VMEM)
    return pl.pallas_call(
        finish_kernel,
        out_shape=jax.ShapeDtypeStruct(diff.shape, F32),
        in_specs=[vmem, vmem],
        out_specs=vmem,
        compiler_params=pltpu.CompilerParams(vmem_limit_bytes=8 * 2**20),
        name="finish",
    )(stats, diff)


def attend(rot_queries, rot_keys, values_new, cache_keys, cache_values, cache_lengths):
    req_dev, slot_count, kv_dev, _ = cache_keys.shape
    group_size = rot_queries.shape[1] // kv_dev
    grouped = rot_queries.reshape(req_dev, kv_dev, group_size, HEAD_DIM)
    scores = jnp.einsum(
        "nkgd,nlkd->nkgl", grouped, cache_keys, preferred_element_type=jnp.float32
    ) / math.sqrt(HEAD_DIM)
    own_score = jnp.einsum(
        "nkgd,nkd->nkg", grouped, rot_keys, preferred_element_type=jnp.float32
    ) / math.sqrt(HEAD_DIM)
    valid_mask = jnp.arange(slot_count)[None, :] < cache_lengths[:, None]
    scores = jnp.where(valid_mask[:, None, None, :], scores, -jnp.inf)
    row_peak = jnp.maximum(jnp.max(scores, axis=-1), own_score)
    expo = jnp.exp(scores - row_peak[..., None])
    own_expo = jnp.exp(own_score - row_peak)
    sum_exp = jnp.sum(expo, axis=-1) + own_expo
    weights = (expo / sum_exp[..., None]).astype(BF)
    own_weight = (own_expo / sum_exp).astype(BF)
    mixed = jnp.einsum("nkgl,nlkd->nkgd", weights, cache_values, preferred_element_type=jnp.float32)
    mixed = mixed + own_weight.astype(F32)[..., None] * values_new.astype(F32)[:, :, None, :]
    return mixed.reshape(req_dev, kv_dev * group_size * HEAD_DIM).astype(BF)


def shards(
    hidden_in,
    attn_gain,
    w_query,
    w_keyval,
    w_output,
    final_gain,
    w_head,
    cache_keys,
    cache_values,
    cache_lengths,
    premature,
    premature_layer,
):
    req_dev, width_all = hidden_in.shape
    plane_size = NX * NZ * NC
    t_pos = lax.axis_index("t")
    c_pos = lax.axis_index("c")
    plane_pos = lax.axis_index(PLANE)
    cols = width_all // plane_size

    head_t = lax.all_gather(w_head, "t", axis=0, tiled=True).T

    both, early_rows = opening_blocks(
        hidden_in, attn_gain, final_gain, premature, premature_layer
    )
    q_both = jnp.concatenate(by_core(w_query, swap_cores(w_query)), axis=0)
    kv_both = jnp.concatenate(by_core(w_keyval, swap_cores(w_keyval)), axis=1)
    w_both = jnp.concatenate([q_both, kv_both[0], kv_both[1]], axis=1)
    both, w_both = lax.optimization_barrier((exchange(both, CHIPS), w_both))
    group = NZ * NC * req_dev
    normed = both[:, :req_dev].reshape(NX * NZ * req_dev, NC * cols)
    hidden_rows = both[:, req_dev:].reshape(NX, NZ, req_dev, NC, cols)
    hidden_rows = lax.dynamic_index_in_dim(hidden_rows, t_pos, 0, keepdims=False)
    hidden_own = lax.dynamic_index_in_dim(hidden_rows, c_pos, 2, keepdims=False)
    hidden_sent = lax.dynamic_index_in_dim(hidden_rows, 1 - c_pos, 2, keepdims=False)
    hidden_rows = jnp.stack(by_core(hidden_own, swap_cores(hidden_sent)), axis=1)
    hidden_rows = hidden_rows.reshape(group, cols)

    slice_width = width_all // NT
    early_part = lax.dynamic_slice_in_dim(early_rows, t_pos * slice_width, slice_width, 1)
    early_part = early_part.reshape(req_dev, NX, slice_width // NX).transpose(1, 0, 2)
    early_quarters = jnp.broadcast_to(early_part[:, None], (NX, NZ) + early_part.shape[1:])
    early_quarters = early_quarters.reshape(NX * NZ, req_dev, slice_width // NX)

    sums = jnp.dot(normed, w_both, preferred_element_type=F32)
    blocks = sums.astype(BF).reshape(NX * NZ, req_dev, w_both.shape[1])
    summed = exchange(jnp.concatenate([blocks, early_quarters], axis=2), CHIPS)
    summed, hidden_rows = lax.optimization_barrier((summed, hidden_rows))
    projected = jnp.sum(summed[:, :, : w_both.shape[1]].astype(F32), axis=0)
    early = lax.all_gather(summed[:, :, w_both.shape[1] :], "x", axis=0)

    query_cols = w_query.shape[1]
    pair_cols = w_keyval.shape[2]
    heads_dev = query_cols // HEAD_DIM
    kv_dev = pair_cols // HEAD_DIM
    queries = projected[:, :query_cols].reshape(req_dev, heads_dev, HEAD_DIM)
    keys_new = projected[:, query_cols : query_cols + pair_cols].reshape(req_dev, kv_dev, HEAD_DIM)
    values_new = (
        projected[:, query_cols + pair_cols :].reshape(req_dev, kv_dev, HEAD_DIM).astype(BF)
    )
    positions = cache_lengths.astype(F32)
    rot_queries = rotate(queries, positions).astype(BF)
    rot_keys = rotate(keys_new, positions).astype(BF)
    attended = attend(rot_queries, rot_keys, values_new, cache_keys, cache_values, cache_lengths)

    own_rows = exchange(jnp.broadcast_to(attended[None], (NX * NZ,) + attended.shape), CHIPS)
    own_rows, early = lax.optimization_barrier((own_rows, early))
    other_rows = swap_cores(own_rows)
    parts = project(c_pos[None], own_rows, other_rows, w_output)
    parts, early = lax.optimization_barrier((parts, early))
    parts = exchange(parts, ("t",))

    early_sums = early_head(c_pos[None], early, swap_cores(early), w_head.T)
    parts, early_sums = lax.optimization_barrier((parts, early_sums))
    early_parts = []
    for k in range(NT):
        block = lax.dynamic_index_in_dim(early_sums, (t_pos + k) % NT, 0, keepdims=False)
        if k > 0:
            block = lax.ppermute(block, "t", [(t, (t + k) % NT) for t in range(NT)])
        early_parts.append(block)

    scaled = settle(plane_pos[None], parts, hidden_rows, final_gain)
    own_cols = exchange(scaled, CHIPS)
    own_cols, *early_parts = lax.optimization_barrier((own_cols, *early_parts))
    other_cols = swap_cores(own_cols)
    gain = final_gain.reshape(plane_size, cols)
    diff, stats = head(c_pos[None], own_cols, other_cols, gain, early_parts, head_t)

    stats = exchange(stats, PLANE)
    return finish(stats, diff)


def solution(mesh):
    fine = Mesh(mesh.devices.reshape(NT, NX, NZ, NC), ("t", "x", "z", "c"))
    placed = (
        P(PLANE, None),
        P(),
        P(PLANE, "t"),
        P(None, PLANE, "t"),
        P("t", PLANE),
        P(),
        P("t", PLANE),
        P(PLANE, None, "t", None),
        P(PLANE, None, "t", None),
        P(PLANE),
        P(None, PLANE, None),
        P(PLANE),
    )
    return jax.shard_map(
        shards, mesh=fine, in_specs=placed, out_specs=P("t", PLANE), check_vma=False
    )
```
